512 devices in a mesh: dp: 32 (over z, y_hi), tensor: 16 (over x, y_lo, core).
Axes of the slice: x: 4, y: 4 (y_hi: 2, y_lo: 2; y = y_hi * 2 + y_lo), z: 16, core: 2. Of those that a mesh axis runs over, the one named last changes fastest.
Arguments:
- gradient: bfloat16 [8192, 28672], P('dp', 'tensor'), may hold values from -5 to 5
- left_codes: bfloat16 [32, 1024, 1024], P('dp', 'tensor'), may hold values from -1 to 1
- left_scales: float32 [32, 1024, 8], P('dp', 'tensor'), may hold values from 0.05 to 0.5
Outputs:
- new_codes: bfloat16 [32, 1024, 1024], P('dp', 'tensor')
- new_scales: float32 [32, 1024, 8], P('dp', 'tensor')
The draws below stay inside these ranges and needn't reach their ends.
All inputs are finite; a program needn't handle non-finite values. Where the reference program divides by a largest or mean magnitude, that divisor is 1e-20 or more.
Results may differ from the reference program's by a relative error of at most 0.001.
Values may be sent and summed in bfloat16 or wider, within the bound.
No kernel may reach another device: no remote copies, remote signals or barrier semaphores. Data moves between devices by JAX's collectives and lax.ppermute only.
A program may use at most 64 MiB of HBM per device.

```python
import math
import jax
import jax.numpy as jnp
from jax import lax

D = 8192
FF = 28672
BLOCK = 4096
GROUP = 128
SIDE = 4
ROWS_DEV = 256
TILE = 1024
OWNERS = 32


def draw_gradient(key, part):
    key = jax.random.fold_in(key, 11)
    key_noise, key_rows = jax.random.split(key, 2)
    row_scale = jnp.exp(jax.random.uniform(key_rows, (D, 1), jnp.float32, math.log(0.3), math.log(3.0)))
    spread = jnp.clip(jax.random.normal(key_noise, (D, FF), jnp.float32), -5.0, 5.0)
    return (spread * row_scale * FF ** (-0.25)).astype(jnp.bfloat16)


def steps_of(stream_key, shape, pieces, smallest, high):
    gain = 1.0
    for position, shards_of in pieces:
        heights = jax.random.uniform(jax.random.fold_in(jax.random.fold_in(stream_key, 6), position), (shards_of,), jnp.float32, smallest / len(pieces), high / len(pieces))
        gain = gain * jnp.repeat(jnp.exp(heights), shape[position] // shards_of).reshape((-1,) + (1,) * (len(shape) - 1 - position))
    return gain


def setup_inputs(seed: int = 0) -> dict:
    keys = jax.random.split(jax.random.key(seed), 4)
    return {
        "gradient": draw_gradient(jax.random.fold_in(keys[3], 71), 0),
        "left_codes": jnp.clip(jax.random.uniform(keys[1], (OWNERS, TILE, TILE), jnp.float32, -1.0, 1.0) * steps_of(keys[1], (OWNERS, TILE, TILE), ((0, 32), (1, 16)), -0.4, 0.0), -1.0, 1.0).astype(jnp.bfloat16),
        "left_scales": jnp.clip(jnp.exp(math.log(0.5) - 2.3025851 * jax.random.uniform(keys[2], (OWNERS, TILE, TILE // GROUP), jnp.float32) ** steps_of(keys[2], (OWNERS, TILE, TILE // GROUP), ((0, 32), (1, 16)), -0.2, 0.2)), 0.05, 0.5),
    }


def hadamard_table(matrix_order):
    index_row = lax.broadcasted_iota(jnp.int32, (matrix_order, matrix_order), 0)
    index_col = lax.broadcasted_iota(jnp.int32, (matrix_order, matrix_order), 1)
    parity = jnp.zeros((matrix_order, matrix_order), jnp.int32)
    for bit_pos in range(matrix_order.bit_length() - 1):
        parity = parity + jnp.right_shift(index_row, bit_pos) % 2 * (jnp.right_shift(index_col, bit_pos) % 2)
    signs = 1.0 - 2.0 * (parity % 2).astype(jnp.float32)
    return signs / jnp.sqrt(jnp.float32(matrix_order))

def rotate(values, hadamard):
    group_size = hadamard.shape[0]
    row_total, col_total = values.shape
    grouped = values.reshape(row_total, col_total // group_size, group_size)
    turned = jnp.einsum('rkn,nm->rkm', grouped, hadamard, precision=lax.Precision.HIGHEST)
    return turned.reshape(row_total, col_total)

def refresh(old_codes, old_scales, gram, hadamard):
    group_size = hadamard.shape[0]
    row_total, col_total = gram.shape
    grouped = old_codes.astype(jnp.float32).reshape(row_total, col_total // group_size, group_size)
    dequant = (grouped * old_scales[:, :, None]).reshape(row_total, col_total)
    old_factor = rotate(dequant, hadamard)
    blended = 0.95 * old_factor + 0.05 * gram
    rotated = rotate(blended, hadamard).reshape(row_total, col_total // group_size, group_size)
    fresh_scales = lax.optimization_barrier(jnp.max(jnp.abs(rotated), axis=2))
    fresh_codes = (rotated / (fresh_scales[:, :, None] + 1e-06)).reshape(row_total, col_total)
    return (fresh_codes.astype(jnp.bfloat16), fresh_scales)

def reference(gradient, left_codes, left_scales):
    hadamard = hadamard_table(GROUP)

    def one_owner(owner):
        block_no = owner // (SIDE * SIDE)
        row_group = owner // SIDE % SIDE
        col_group = owner % SIDE
        block_rows = lax.dynamic_slice_in_dim(gradient, (block_no * BLOCK).astype(jnp.int32), BLOCK, 0)
        tile_rows = lax.dynamic_slice_in_dim(block_rows, (row_group * TILE).astype(jnp.int32), TILE, 0)
        shaped = block_rows.reshape(SIDE, SIDE, ROWS_DEV, FF)
        tile_cols = lax.dynamic_index_in_dim(shaped, col_group.astype(jnp.int32), 1, keepdims=False).reshape(TILE, FF)
        gram = lax.dot_general(tile_rows, tile_cols, (((1,), (1,)), ((), ())), preferred_element_type=jnp.float32)
        return refresh(left_codes[owner], left_scales[owner], gram, hadamard)
    new_codes, new_scales = lax.map(one_owner, jnp.arange(OWNERS, dtype=jnp.int32))
    return (new_codes, new_scales)
```

```python
import jax
import jax.numpy as jnp
from jax import lax
from jax.sharding import PartitionSpec as P

GROUP = 128
AXES = ("dp", "tensor")
SUPERS = 4


def place(index):
    dp, tensor = divmod(index, 16)
    return dict(
        b=dp >> 4, g=(dp >> 2) & 3, h=dp & 3, x=tensor >> 2, yl=(tensor >> 1) & 1, c=tensor & 1
    )


def index_of(b, g, h, x, yl, c):
    return ((b << 4 | g << 2 | h) << 4) | x << 2 | yl << 1 | c


def permute(array, target, keep=lambda at: True):
    total = lax.axis_size("dp") * lax.axis_size("tensor")
    pairs = []
    for i in range(total):
        at = place(i)
        if keep(at):
            pairs.append((i, index_of(**{**at, **target(at)})))
    return lax.ppermute(array, AXES, pairs)


def reach(at):
    return at["g"] if at["c"] == 0 else SUPERS - 1 - at["g"]


def onward(at):
    return dict(g=at["g"] + (1 if at["c"] == 0 else -1))


def hadamard_table(matrix_order):
    index_row = lax.broadcasted_iota(jnp.int32, (matrix_order, matrix_order), 0)
    index_col = lax.broadcasted_iota(jnp.int32, (matrix_order, matrix_order), 1)
    parity = jnp.zeros((matrix_order, matrix_order), jnp.int32)
    for bit_pos in range(matrix_order.bit_length() - 1):
        parity = parity + jnp.right_shift(index_row, bit_pos) % 2 * (
            jnp.right_shift(index_col, bit_pos) % 2
        )
    signs = 1.0 - 2.0 * (parity % 2).astype(jnp.float32)
    return signs / jnp.sqrt(jnp.float32(matrix_order))


def refresh(old_codes, old_scales, gram, hadamard):
    rows, cols = gram.shape
    groups = cols // GROUP
    grouped = gram.reshape(rows, groups, GROUP)
    turned = jnp.einsum("rkn,nm->rkm", grouped, hadamard, precision=lax.Precision.HIGHEST)
    dequant = old_codes.astype(jnp.float32).reshape(rows, groups, GROUP) * old_scales[:, :, None]
    rotated = 0.95 * dequant + 0.05 * turned
    fresh_scales = jnp.max(jnp.abs(rotated), axis=2)
    fresh_codes = (rotated / (fresh_scales[:, :, None] + 1e-06)).reshape(rows, cols)
    return fresh_codes.astype(jnp.bfloat16), fresh_scales


def swap_if(flag, first, second):
    return jnp.where(flag, second, first), jnp.where(flag, first, second)


def per_device(gradient, left_codes, left_scales):
    dp, tensor = lax.axis_index("dp"), lax.axis_index("tensor")
    g, h = (dp >> 2) & 3, dp & 3
    x, yl, c = tensor >> 2, (tensor >> 1) & 1, tensor & 1
    block = gradient.shape[0]
    half, quarter = block // 2, block // 4

    passing = [gradient]
    for step in range(1, SUPERS):
        passing.append(
            permute(
                passing[-1],
                onward,
                lambda at, step=step: step - 1 <= reach(at) < SUPERS - 1,
            )
        )

    z_block = permute(gradient, lambda at: dict(h=at["h"] ^ 2))
    y_block = permute(gradient, lambda at: dict(h=at["h"] ^ 1))
    zy_block = permute(z_block, lambda at: dict(h=at["h"] ^ 1))
    turn = x ^ h
    low = swap_if(turn & 1 == 1, gradient, y_block)
    high = swap_if(turn & 1 == 1, z_block, zy_block)
    s0, s2 = swap_if(turn >> 1 == 1, low[0], high[0])
    s1, s3 = swap_if(turn >> 1 == 1, low[1], high[1])
    stationary = [s0, s1, s2, s3]

    def product(rows, cols):
        return lax.dot_general(
            rows, cols, (((1,), (1,)), ((), ())), preferred_element_type=jnp.float32
        )

    sums = [None] * SUPERS
    for steps in ((0, 1), (2,), (3,)):
        parts = [
            jnp.stack([product(rows, passing[step]) for step in steps]) for rows in stationary
        ]
        valid = lambda at, steps=steps: reach(at) >= steps[0]
        total = parts[0]
        for d in (1, 3, 2):
            total = total + permute(parts[d], lambda at, d=d: dict(x=at["x"] ^ d), valid)
        keep = lax.dynamic_slice_in_dim(total, yl * half, half, 1)
        give = lax.dynamic_slice_in_dim(total, (1 - yl) * half, half, 1)
        done = keep + permute(give, lambda at: dict(yl=at["yl"] ^ 1), valid)
        for k, step in enumerate(steps):
            sums[step] = done[k]

    every = jnp.stack(sums)
    own = lax.dynamic_slice_in_dim(every, c * quarter, quarter, 1)
    other = permute(
        lax.dynamic_slice_in_dim(every, (1 - c) * quarter, quarter, 1),
        lambda at: dict(c=at["c"] ^ 1),
    )
    first = c == 0
    offsets = [
        own[0] + other[0],
        jnp.where(first, other[1] + own[3], own[1] + other[3]),
        own[2] + other[2],
        jnp.where(first, own[1] + other[3], other[1] + own[3]),
    ]

    across = [None]
    for step in range(1, SUPERS):
        across.append(
            permute(
                sums[step],
                lambda at, step=step: dict(
                    g=at["g"] + (-step if at["c"] == 0 else step), h=at["x"], x=at["h"]
                ),
                lambda at, step=step: reach(at) >= step,
            )
        )
    flipped = jnp.stack(
        [
            jnp.where(first, across[1], across[3]).T,
            across[2].T,
            jnp.where(first, across[3], across[1]).T,
        ]
    )
    pieces = lax.all_to_all(
        flipped.reshape(3, 4, quarter, half),
        "tensor",
        1,
        1,
        axis_index_groups=[[4 * i + k for k in range(4)] for i in range(4)],
        tiled=True,
    ).reshape(3, 2, 2, quarter, half)
    pieces = pieces[:, :, 0] + pieces[:, :, 1]
    for step in range(1, SUPERS):
        offsets[step] = offsets[step] + jnp.concatenate(
            [pieces[step - 1, 0], pieces[step - 1, 1]], axis=1
        )
    around = jnp.concatenate(offsets + offsets[:-1], axis=1)
    gram = lax.dynamic_slice_in_dim(around, (SUPERS - g) % SUPERS * block, SUPERS * block, 1)
    fresh_codes, fresh_scales = refresh(left_codes[0], left_scales[0], gram, hadamard_table(GROUP))
    return fresh_codes[None], fresh_scales[None]


def solution(mesh):
    return jax.shard_map(
        per_device,
        mesh=mesh,
        in_specs=(P("dp", "tensor"), P("dp", "tensor", None), P("dp", "tensor", None)),
        out_specs=(P("dp", "tensor", None), P("dp", "tensor", None)),
        check_vma=False,
    )
```

```python
import jax
import jax.numpy as jnp
from jax import lax
from jax.sharding import PartitionSpec as P

GROUP = 128
AXES = ("dp", "tensor")
SUPERS = 4


def place(index):
    dp, tensor = divmod(index, 16)
    return dict(
        b=dp >> 4, g=(dp >> 2) & 3, h=dp & 3, x=tensor >> 2, yl=(tensor >> 1) & 1, c=tensor & 1
    )


def index_of(b, g, h, x, yl, c):
    return ((b << 4 | g << 2 | h) << 4) | x << 2 | yl << 1 | c


def permute(array, target, keep=lambda at: True):
    total = lax.axis_size("dp") * lax.axis_size("tensor")
    pairs = []
    for i in range(total):
        at = place(i)
        if keep(at):
            pairs.append((i, index_of(**{**at, **target(at)})))
    return lax.ppermute(array, AXES, pairs)


def reach(at):
    return at["g"] if at["c"] == 0 else SUPERS - 1 - at["g"]


def onward(at):
    return dict(g=at["g"] + (1 if at["c"] == 0 else -1))


def hadamard_table(matrix_order):
    index_row = lax.broadcasted_iota(jnp.int32, (matrix_order, matrix_order), 0)
    index_col = lax.broadcasted_iota(jnp.int32, (matrix_order, matrix_order), 1)
    parity = jnp.zeros((matrix_order, matrix_order), jnp.int32)
    for bit_pos in range(matrix_order.bit_length() - 1):
        parity = parity + jnp.right_shift(index_row, bit_pos) % 2 * (
            jnp.right_shift(index_col, bit_pos) % 2
        )
    signs = 1.0 - 2.0 * (parity % 2).astype(jnp.float32)
    return signs / jnp.sqrt(jnp.float32(matrix_order))


def refresh(old_codes, old_scales, gram, hadamard):
    rows, cols = gram.shape
    groups = cols // GROUP
    grouped = gram.reshape(rows, groups, GROUP)
    turned = jnp.einsum("rkn,nm->rkm", grouped, hadamard, precision=lax.Precision.HIGHEST)
    dequant = old_codes.astype(jnp.float32).reshape(rows, groups, GROUP) * old_scales[:, :, None]
    rotated = 0.95 * dequant + 0.05 * turned
    fresh_scales = jnp.max(jnp.abs(rotated), axis=2)
    fresh_codes = (rotated / (fresh_scales[:, :, None] + 1e-06)).reshape(rows, cols)
    return fresh_codes.astype(jnp.bfloat16), fresh_scales


def swap_if(flag, first, second):
    return jnp.where(flag, second, first), jnp.where(flag, first, second)


def per_device(gradient, left_codes, left_scales):
    dp, tensor = lax.axis_index("dp"), lax.axis_index("tensor")
    g, h = (dp >> 2) & 3, dp & 3
    x, yl, c = tensor >> 2, (tensor >> 1) & 1, tensor & 1
    block = gradient.shape[0]
    half, quarter = block // 2, block // 4

    passing = [gradient]
    for step in range(1, SUPERS):
        passing.append(
            permute(
                passing[-1],
                onward,
                lambda at, step=step: step - 1 <= reach(at) < SUPERS - 1,
            )
        )

    z_block = permute(gradient, lambda at: dict(h=at["h"] ^ 2))
    y_block = permute(gradient, lambda at: dict(h=at["h"] ^ 1))
    zy_block = permute(z_block, lambda at: dict(h=at["h"] ^ 1))
    turn = x ^ h
    low = swap_if(turn & 1 == 1, gradient, y_block)
    high = swap_if(turn & 1 == 1, z_block, zy_block)
    s0, s2 = swap_if(turn >> 1 == 1, low[0], high[0])
    s1, s3 = swap_if(turn >> 1 == 1, low[1], high[1])
    stationary = [s0, s1, s2, s3]

    def product(rows, cols):
        return lax.dot_general(
            rows, cols, (((1,), (1,)), ((), ())), preferred_element_type=jnp.float32
        )

    def half_of(array, flag, size, axis):
        return lax.dynamic_slice_in_dim(array, flag * size, size, axis)

    own, across = [None] * SUPERS, [None] * SUPERS
    for steps in ((0, 1), (2, 3)):
        parts = [
            jnp.stack([product(rows, passing[step]) for step in steps]) for rows in stationary
        ]
        valid = lambda at, steps=steps: reach(at) >= steps[0]
        total = parts[0]
        for d in (1, 3, 2):
            total = total + permute(parts[d], lambda at, d=d: dict(x=at["x"] ^ d), valid)
        far = [k for k, step in enumerate(steps) if step]
        both = jnp.stack(list(total) + [total[k].T for k in far])
        done = half_of(both, yl, half, 1) + permute(
            half_of(both, 1 - yl, half, 1), lambda at: dict(yl=at["yl"] ^ 1), valid
        )
        for k, step in enumerate(steps):
            own[step] = done[k]
        for k, place_no in enumerate(far):
            step = steps[place_no]
            across[step] = permute(
                done[len(steps) + k],
                lambda at, step=step: dict(
                    g=at["g"] + (-step if at["c"] == 0 else step), h=at["x"], x=at["h"]
                ),
                lambda at, step=step: reach(at) >= step,
            )

    first = c == 0
    strips = jnp.stack(
        [
            own[0],
            jnp.where(first, own[3] + across[1], own[1] + across[3]),
            own[2] + across[2],
            jnp.where(first, own[1] + across[3], own[3] + across[1]),
        ]
    )
    offsets = half_of(strips, c, quarter, 1) + permute(
        half_of(strips, 1 - c, quarter, 1), lambda at: dict(c=at["c"] ^ 1)
    )
    offsets = list(offsets)
    around = jnp.concatenate(offsets + offsets[:-1], axis=1)
    gram = lax.dynamic_slice_in_dim(around, (SUPERS - g) % SUPERS * block, SUPERS * block, 1)
    fresh_codes, fresh_scales = refresh(left_codes[0], left_scales[0], gram, hadamard_table(GROUP))
    return fresh_codes[None], fresh_scales[None]


def solution(mesh):
    return jax.shard_map(
        per_device,
        mesh=mesh,
        in_specs=(P("dp", "tensor"), P("dp", "tensor", None), P("dp", "tensor", None)),
        out_specs=(P("dp", "tensor", None), P("dp", "tensor", None)),
        check_vma=False,
    )
```

```python
import jax
import jax.numpy as jnp
from jax import lax
from jax.sharding import PartitionSpec as P

GROUP = 128
AXES = ("dp", "tensor")
SUPERS = 4


def place(index):
    dp, tensor = divmod(index, 16)
    return dict(
        b=dp >> 4, g=(dp >> 2) & 3, h=dp & 3, x=tensor >> 2, yl=(tensor >> 1) & 1, c=tensor & 1
    )


def index_of(b, g, h, x, yl, c):
    return ((b << 4 | g << 2 | h) << 4) | x << 2 | yl << 1 | c


def permute(array, target, keep=lambda at: True):
    total = lax.axis_size("dp") * lax.axis_size("tensor")
    pairs = []
    for i in range(total):
        at = place(i)
        if keep(at):
            pairs.append((i, index_of(**{**at, **target(at)})))
    return lax.ppermute(array, AXES, pairs)


def reach(at):
    return at["g"] if at["c"] == 0 else SUPERS - 1 - at["g"]


def onward(at):
    return dict(g=at["g"] + (1 if at["c"] == 0 else -1))


def hadamard_table(matrix_order):
    index_row = lax.broadcasted_iota(jnp.int32, (matrix_order, matrix_order), 0)
    index_col = lax.broadcasted_iota(jnp.int32, (matrix_order, matrix_order), 1)
    parity = jnp.zeros((matrix_order, matrix_order), jnp.int32)
    for bit_pos in range(matrix_order.bit_length() - 1):
        parity = parity + jnp.right_shift(index_row, bit_pos) % 2 * (
            jnp.right_shift(index_col, bit_pos) % 2
        )
    signs = 1.0 - 2.0 * (parity % 2).astype(jnp.float32)
    return signs / jnp.sqrt(jnp.float32(matrix_order))


def refresh(old_codes, old_scales, gram, hadamard):
    rows, cols = gram.shape
    groups = cols // GROUP
    grouped = gram.reshape(rows, groups, GROUP)
    turned = jnp.einsum("rkn,nm->rkm", grouped, hadamard, precision=lax.Precision.HIGHEST)
    dequant = old_codes.astype(jnp.float32).reshape(rows, groups, GROUP) * old_scales[:, :, None]
    rotated = 0.95 * dequant + 0.05 * turned
    fresh_scales = jnp.max(jnp.abs(rotated), axis=2)
    fresh_codes = (rotated / (fresh_scales[:, :, None] + 1e-06)).reshape(rows, cols)
    return fresh_codes.astype(jnp.bfloat16), fresh_scales


def swap_if(flag, first, second):
    return jnp.where(flag, second, first), jnp.where(flag, first, second)


def per_device(gradient, left_codes, left_scales):
    dp, tensor = lax.axis_index("dp"), lax.axis_index("tensor")
    g, h = (dp >> 2) & 3, dp & 3
    x, yl, c = tensor >> 2, (tensor >> 1) & 1, tensor & 1
    block = gradient.shape[0]
    half, quarter = block // 2, block // 4

    passing = [gradient]
    for step in range(1, SUPERS):
        passing.append(
            permute(
                passing[-1],
                onward,
                lambda at, step=step: step - 1 <= reach(at) < SUPERS - 1,
            )
        )

    z_block = permute(gradient, lambda at: dict(h=at["h"] ^ 2))
    y_block = permute(gradient, lambda at: dict(h=at["h"] ^ 1))
    zy_block = permute(z_block, lambda at: dict(h=at["h"] ^ 1))
    turn = x ^ h
    low = swap_if(turn & 1 == 1, gradient, y_block)
    high = swap_if(turn & 1 == 1, z_block, zy_block)
    s0, s2 = swap_if(turn >> 1 == 1, low[0], high[0])
    s1, s3 = swap_if(turn >> 1 == 1, low[1], high[1])
    stationary = [s0, s1, s2, s3]

    def product(rows, cols):
        return lax.dot_general(
            rows, cols, (((1,), (1,)), ((), ())), preferred_element_type=jnp.float32
        )

    def half_of(array, flag, size, axis):
        return lax.dynamic_slice_in_dim(array, flag * size, size, axis)

    own, across = [None] * SUPERS, [None] * SUPERS
    for steps in ((0, 1), (2,), (3,)):
        parts = [
            jnp.stack([product(rows, passing[step]) for step in steps]) for rows in stationary
        ]
        valid = lambda at, steps=steps: reach(at) >= steps[0]
        total = parts[0]
        for d in (1, 3, 2):
            total = total + permute(parts[d], lambda at, d=d: dict(x=at["x"] ^ d), valid)
        if steps[-1] < SUPERS - 1:
            ahead = steps[-1] + 1
            passing[ahead], total = lax.optimization_barrier((passing[ahead], total))
        far = [k for k, step in enumerate(steps) if step]
        both = jnp.stack(list(total) + [total[k].T for k in far])
        done = half_of(both, yl, half, 1) + permute(
            half_of(both, 1 - yl, half, 1), lambda at: dict(yl=at["yl"] ^ 1), valid
        )
        for k, step in enumerate(steps):
            own[step] = done[k]
        for k, place_no in enumerate(far):
            step = steps[place_no]
            across[step] = permute(
                done[len(steps) + k],
                lambda at, step=step: dict(
                    g=at["g"] + (-step if at["c"] == 0 else step), h=at["x"], x=at["h"]
                ),
                lambda at, step=step: reach(at) >= step,
            )

    first = c == 0
    strips = jnp.stack(
        [
            own[0],
            jnp.where(first, own[3] + across[1], own[1] + across[3]),
            own[2] + across[2],
            jnp.where(first, own[1] + across[3], own[3] + across[1]),
        ]
    )
    offsets = half_of(strips, c, quarter, 1) + permute(
        half_of(strips, 1 - c, quarter, 1), lambda at: dict(c=at["c"] ^ 1)
    )
    offsets = list(offsets)
    around = jnp.concatenate(offsets + offsets[:-1], axis=1)
    gram = lax.dynamic_slice_in_dim(around, (SUPERS - g) % SUPERS * block, SUPERS * block, 1)
    fresh_codes, fresh_scales = refresh(left_codes[0], left_scales[0], gram, hadamard_table(GROUP))
    return fresh_codes[None], fresh_scales[None]


def solution(mesh):
    return jax.shard_map(
        per_device,
        mesh=mesh,
        in_specs=(P("dp", "tensor"), P("dp", "tensor", None), P("dp", "tensor", None)),
        out_specs=(P("dp", "tensor", None), P("dp", "tensor", None)),
        check_vma=False,
    )
```

```python
import functools

import jax
import jax.numpy as jnp
from jax import lax
from jax.experimental import pallas as pl
from jax.experimental.pallas import tpu as pltpu
from jax.sharding import PartitionSpec as P

GROUP = 128
AXES = ("dp", "tensor")
SUPERS = 4
VMEM = pl.BlockSpec(memory_space=pltpu.VMEM)
SMEM = pl.BlockSpec(memory_space=pltpu.SMEM)


def place(index):
    dp, tensor = divmod(index, 16)
    return dict(
        b=dp >> 4, g=(dp >> 2) & 3, h=dp & 3, x=tensor >> 2, yl=(tensor >> 1) & 1, c=tensor & 1
    )


def index_of(b, g, h, x, yl, c):
    return ((b << 4 | g << 2 | h) << 4) | x << 2 | yl << 1 | c


def permute(array, target, keep=lambda at: True):
    total = lax.axis_size("dp") * lax.axis_size("tensor")
    pairs = []
    for i in range(total):
        at = place(i)
        if keep(at):
            pairs.append((i, index_of(**{**at, **target(at)})))
    return lax.ppermute(array, AXES, pairs)


def reach(at):
    return at["g"] if at["c"] == 0 else SUPERS - 1 - at["g"]


def onward(at):
    return dict(g=at["g"] + (1 if at["c"] == 0 else -1))


def call(kernel, name, outs, flops, *operands):
    in_specs = [SMEM if op.dtype == jnp.int32 else VMEM for op in operands]
    moved = sum(op.size * op.dtype.itemsize for op in (*operands, *outs))
    return pl.pallas_call(
        kernel,
        out_shape=outs,
        in_specs=in_specs,
        out_specs=[VMEM] * len(outs),
        compiler_params=pltpu.CompilerParams(vmem_limit_bytes=40 * 1024 * 1024),
        cost_estimate=pl.CostEstimate(flops=flops, bytes_accessed=moved, transcendentals=0),
        name=name,
    )(*operands)


def floats(*shape):
    return jax.ShapeDtypeStruct(shape, jnp.float32)


def products_kernel(where, *refs):
    rows, cols, outs = refs[:4], refs[4:-4], refs[-4:]
    for turn in range(4):

        @pl.when(where[0] == turn)
        def _():
            for d in range(4):
                for k, col in enumerate(cols):
                    outs[d][k] = lax.dot_general(
                        rows[d ^ turn][...],
                        col[...],
                        (((1,), (1,)), ((), ())),
                        preferred_element_type=jnp.float32,
                    )


def products(where, rows, cols):
    size, depth = rows[0].shape
    count = len(cols)
    return call(
        products_kernel,
        "block_products",
        [floats(count, size, size)] * 4,
        8 * count * size * size * depth,
        where,
        *rows,
        *cols,
    )


def halves_kernel(far, where, first, second, third, fourth, keep, give):
    count, size, _ = first.shape
    half = size // 2
    upper = where[1] == 1
    totals = [first[k] + second[k] + third[k] + fourth[k] for k in range(count)]
    for k, total in enumerate(totals + [totals[k].T for k in far]):
        keep[k] = jnp.where(upper, total[half:], total[:half])
        give[k] = jnp.where(upper, total[:half], total[half:])


def halves(where, far, parts):
    count, size, _ = parts[0].shape
    shape = floats(count + len(far), size // 2, size)
    return call(
        functools.partial(halves_kernel, far), "halves", [shape, shape], 0, where, *parts
    )


def strips_kernel(where, *refs):
    own, across, keep, give = refs[:4], (None, *refs[4:7]), refs[7], refs[8]
    half = keep.shape[1]
    second = where[2] == 1
    back = own[3][...] + across[1][...], own[1][...] + across[3][...]
    strips = [
        own[0][...],
        jnp.where(second, back[1], back[0]),
        own[2][...] + across[2][...],
        jnp.where(second, back[0], back[1]),
    ]
    for k, strip in enumerate(strips):
        keep[k] = jnp.where(second, strip[half:], strip[:half])
        give[k] = jnp.where(second, strip[:half], strip[half:])


def strips(where, own, across):
    rows, cols = own[0].shape
    shape = floats(SUPERS, rows // 2, cols)
    return call(strips_kernel, "strips", [shape, shape], 0, where, *own, *across)


def refresh_kernel(where, mine, other, codes, scales, new_codes, new_scales):
    bits = lax.broadcasted_iota(jnp.int32, (GROUP, GROUP), 0) & lax.broadcasted_iota(
        jnp.int32, (GROUP, GROUP), 1
    )
    for shift in (4, 2, 1):
        bits = bits ^ (bits >> shift)
    signs = 1.0 - 2.0 * (bits & 1).astype(jnp.float32)
    unit = 1.0 / (GROUP**0.5)
    per_block = mine.shape[2] // GROUP
    largest = []
    for j in range(SUPERS):
        offset = (j + SUPERS - where[3]) & (SUPERS - 1)
        block = mine[offset] + other[offset]
        for k in range(per_block):
            group = j * per_block + k
            at = slice(group * GROUP, (group + 1) * GROUP)
            turned = jnp.dot(
                block[:, k * GROUP : (k + 1) * GROUP],
                signs,
                precision=lax.Precision.HIGHEST,
                preferred_element_type=jnp.float32,
            )
            old = codes[:, at].astype(jnp.float32) * scales[:, group : group + 1]
            rotated = 0.95 * old + 0.05 * (turned * unit)
            peak = jnp.max(jnp.abs(rotated), axis=1, keepdims=True)
            new_codes[:, at] = (rotated / (peak + 1e-06)).astype(jnp.bfloat16)
            largest.append(peak)
    new_scales[...] = jnp.concatenate(largest, axis=1)


def refresh(where, mine, other, codes, scales):
    return call(
        refresh_kernel,
        "refresh",
        [
            jax.ShapeDtypeStruct(codes.shape, jnp.bfloat16),
            jax.ShapeDtypeStruct(scales.shape, jnp.float32),
        ],
        2 * codes.size * GROUP,
        where,
        mine,
        other,
        codes,
        scales,
    )


def per_device(gradient, left_codes, left_scales):
    dp, tensor = lax.axis_index("dp"), lax.axis_index("tensor")
    where = jnp.stack(
        [(tensor >> 2) ^ (dp & 3), (tensor >> 1) & 1, tensor & 1, (dp >> 2) & 3]
    ).astype(jnp.int32)

    z_block = permute(gradient, lambda at: dict(h=at["h"] ^ 2))
    y_block = permute(gradient, lambda at: dict(h=at["h"] ^ 1))
    z_block, y_block, sent = lax.optimization_barrier((z_block, y_block, gradient))
    zy_block = permute(z_block, lambda at: dict(h=at["h"] ^ 1))
    rows = [gradient, y_block, z_block, zy_block]

    def onwards(block, step):
        return permute(block, onward, lambda at: step - 1 <= reach(at) < SUPERS - 1)

    passing = [sent, onwards(sent, 1)]
    passing[1], rows[3] = lax.optimization_barrier((passing[1], rows[3]))
    passing.append(onwards(passing[1], 2))

    own, across = [None] * SUPERS, [None] * SUPERS
    for steps in ((0, 1), (2,), (3,)):
        parts = list(products(where, rows, [passing[step] for step in steps]))
        valid = lambda at, steps=steps: reach(at) >= steps[0]
        parts[1:] = [
            permute(parts[d], lambda at, d=d: dict(x=at["x"] ^ d), valid) for d in (1, 2, 3)
        ]
        if steps[0] == 0:
            passing[2], *parts = lax.optimization_barrier((passing[2], *parts))
            passing.append(onwards(passing[2], 3))
        far = [k for k, step in enumerate(steps) if step]
        keep, give = halves(where, far, parts)
        if steps[-1] < SUPERS - 1:
            ahead = steps[-1] + 1
            passing[ahead], keep, give = lax.optimization_barrier((passing[ahead], keep, give))
        came = permute(give, lambda at: dict(yl=at["yl"] ^ 1), valid)
        for k, step in enumerate(steps):
            own[step] = keep[k] + came[k]
        for k, place_no in enumerate(far, len(steps)):
            step = steps[place_no]
            across[step] = permute(
                keep[k] + came[k],
                lambda at, step=step: dict(
                    g=at["g"] + (-step if at["c"] == 0 else step), h=at["x"], x=at["h"]
                ),
                lambda at, step=step: reach(at) >= step,
            )

    mine, given = strips(where, own, across[1:])
    other = permute(given, lambda at: dict(c=at["c"] ^ 1))
    fresh_codes, fresh_scales = refresh(where, mine, other, left_codes[0], left_scales[0])
    return fresh_codes[None], fresh_scales[None]


def solution(mesh):
    return jax.shard_map(
        per_device,
        mesh=mesh,
        in_specs=(P("dp", "tensor"), P("dp", "tensor", None), P("dp", "tensor", None)),
        out_specs=(P("dp", "tensor", None), P("dp", "tensor", None)),
        check_vma=False,
    )
```

```python
import functools

import jax
import jax.numpy as jnp
from jax import lax
from jax.experimental import pallas as pl
from jax.experimental.pallas import tpu as pltpu
from jax.sharding import PartitionSpec as P

GROUP = 128
AXES = ("dp", "tensor")
SUPERS = 4
VMEM = pl.BlockSpec(memory_space=pltpu.VMEM)
SMEM = pl.BlockSpec(memory_space=pltpu.SMEM)


def place(index):
    dp, tensor = divmod(index, 16)
    return dict(
        b=dp >> 4, g=(dp >> 2) & 3, h=dp & 3, x=tensor >> 2, yl=(tensor >> 1) & 1, c=tensor & 1
    )


def index_of(b, g, h, x, yl, c):
    return ((b << 4 | g << 2 | h) << 4) | x << 2 | yl << 1 | c


def permute(array, target, keep=lambda at: True):
    total = lax.axis_size("dp") * lax.axis_size("tensor")
    pairs = []
    for i in range(total):
        at = place(i)
        if keep(at):
            pairs.append((i, index_of(**{**at, **target(at)})))
    return lax.ppermute(array, AXES, pairs)


def way(at):
    return 1 if at["c"] == 0 else -1


def reach(at):
    return at["g"] if at["c"] == 0 else SUPERS - 1 - at["g"]


def rank(at):
    z = at["g"] * 2 + (at["h"] >> 1)
    return z if at["c"] == 0 else 2 * SUPERS - 1 - z


def along(at, hops):
    z = at["g"] * 2 + (at["h"] >> 1) + way(at) * hops
    return dict(g=z >> 1, h=(z & 1) << 1 | at["h"] & 1)


def call(kernel, name, outs, flops, *operands, scratch=()):
    in_specs = [SMEM if op.dtype == jnp.int32 else VMEM for op in operands]
    moved = sum(op.size * op.dtype.itemsize for op in (*operands, *outs))
    return pl.pallas_call(
        kernel,
        out_shape=outs,
        in_specs=in_specs,
        out_specs=[VMEM] * len(outs),
        scratch_shapes=list(scratch),
        compiler_params=pltpu.CompilerParams(vmem_limit_bytes=40 * 1024 * 1024),
        cost_estimate=pl.CostEstimate(flops=flops, bytes_accessed=moved, transcendentals=0),
        name=name,
    )(*operands)


def floats(*shape):
    return jax.ShapeDtypeStruct(shape, jnp.float32)


def products_kernel(plan, where, *refs):
    count = len(plan)
    ins, outs, other = refs[:-5], refs[-5:-1], refs[-1]
    for k, (_, _, near, far) in enumerate(plan):
        for flag, number in ((0, near), (1, far)):

            @pl.when(where[1] == flag)
            def _(k=k, number=number):
                other[k] = jnp.zeros_like(other[k]) if number is None else ins[number][...]

    for turn in range(4):

        @pl.when(where[0] == turn)
        def _(turn=turn):
            for d in range(4):
                v = d ^ turn
                for k, (pair, equal, _, _) in enumerate(plan):
                    outs[d][k] = lax.dot_general(
                        ins[pair[v & 1]][...],
                        other[k] if v >> 1 else ins[equal][...],
                        (((1,), (1,)), ((), ())),
                        preferred_element_type=jnp.float32,
                    )


def products(where, plan, blocks):
    size, depth = blocks[0].shape
    count = len(plan)
    return list(
        call(
            functools.partial(products_kernel, plan),
            "block_products",
            [floats(count, size, size)] * 4,
            8 * count * size * size * depth,
            where,
            *blocks,
            scratch=[pltpu.VMEM((count, size, depth), jnp.bfloat16)],
        )
    )


def halves_kernel(where, first, second, third, fourth, keep, give):
    count, size, _ = first.shape
    half = size // 2
    upper = where[2] == 1
    totals = [first[k] + second[k] + third[k] + fourth[k] for k in range(count)]
    for k, total in enumerate(totals + [total.T for total in totals]):
        keep[k] = jnp.where(upper, total[half:], total[:half])
        give[k] = jnp.where(upper, total[:half], total[half:])


def halves(where, parts):
    count, size, _ = parts[0].shape
    shape = floats(2 * count, size // 2, size)
    return call(halves_kernel, "halves", [shape, shape], 0, where, *parts)


def strips_kernel(where, *refs):
    here, there, across, keep, give = refs[:3], refs[3:7], refs[7:11], refs[11], refs[12]
    half = keep.shape[1]
    stays, second = where[5] == 1, where[3] == 1
    own = [jnp.where(stays, here[k][...], there[k][...]) for k in range(3)] + [there[3][...]]
    back = own[3] + across[1][...], own[1] + across[3][...]
    strips = [
        own[0] + across[0][...],
        jnp.where(second, back[1], back[0]),
        own[2] + across[2][...],
        jnp.where(second, back[0], back[1]),
    ]
    for k, strip in enumerate(strips):
        keep[k] = jnp.where(second, strip[half:], strip[:half])
        give[k] = jnp.where(second, strip[:half], strip[half:])


def strips(where, here, there, across):
    rows, cols = here[0].shape
    shape = floats(SUPERS, rows // 2, cols)
    return call(strips_kernel, "strips", [shape, shape], 0, where, *here, *there, *across)


def refresh_kernel(where, mine, other, codes, scales, new_codes, new_scales):
    bits = lax.broadcasted_iota(jnp.int32, (GROUP, GROUP), 0) & lax.broadcasted_iota(
        jnp.int32, (GROUP, GROUP), 1
    )
    for shift in (4, 2, 1):
        bits = bits ^ (bits >> shift)
    signs = 1.0 - 2.0 * (bits & 1).astype(jnp.float32)
    unit = 1.0 / (GROUP**0.5)
    per_block = mine.shape[2] // GROUP
    largest = []
    for j in range(SUPERS):
        offset = (j + SUPERS - where[4]) & (SUPERS - 1)
        block = mine[offset] + other[offset]
        for k in range(per_block):
            group = j * per_block + k
            at = slice(group * GROUP, (group + 1) * GROUP)
            turned = jnp.dot(
                block[:, k * GROUP : (k + 1) * GROUP],
                signs,
                precision=lax.Precision.HIGHEST,
                preferred_element_type=jnp.float32,
            )
            old = codes[:, at].astype(jnp.float32) * scales[:, group : group + 1]
            rotated = 0.95 * old + 0.05 * (turned * unit)
            peak = jnp.max(jnp.abs(rotated), axis=1, keepdims=True)
            new_codes[:, at] = (rotated / (peak + 1e-06)).astype(jnp.bfloat16)
            largest.append(peak)
    new_scales[...] = jnp.concatenate(largest, axis=1)


def refresh(where, mine, other, codes, scales):
    return call(
        refresh_kernel,
        "refresh",
        [
            jax.ShapeDtypeStruct(codes.shape, jnp.bfloat16),
            jax.ShapeDtypeStruct(scales.shape, jnp.float32),
        ],
        2 * codes.size * GROUP,
        where,
        mine,
        other,
        codes,
        scales,
    )


def step_on(block, step):
    def needed(at):
        to = rank(at) + 1
        return to < 2 * SUPERS and step <= to and (step < 5 or to & 1 == 1)

    return permute(block, lambda at: along(at, 1), needed)


def per_device(gradient, left_codes, left_scales):
    dp, tensor = lax.axis_index("dp"), lax.axis_index("tensor")
    turn = (tensor >> 2) ^ (dp & 3)
    core = tensor & 1
    where = jnp.stack(
        [
            turn,
            ((dp >> 1) & 1) ^ core,
            (tensor >> 1) & 1,
            core,
            (dp >> 2) & 3,
            1 - (turn >> 1),
        ]
    ).astype(jnp.int32)

    y_swap = lambda at: dict(h=at["h"] ^ 1)
    y_block = permute(gradient, y_swap)
    passing = [gradient, step_on(gradient, 1)]
    start, passing[1] = lax.optimization_barrier((gradient, passing[1]))
    end_block = permute(start, lambda at: along(at, -2), lambda at: rank(at) >= 6)
    end_y_block = permute(end_block, y_swap, lambda at: rank(at) in (4, 5))
    passing.append(step_on(passing[1], 2))
    passing[2], y_block = lax.optimization_barrier((passing[2], y_block))
    passing.append(step_on(passing[2], 3))
    passing[3], end_block = lax.optimization_barrier((passing[3], end_block))
    passing.append(step_on(passing[3], 4))

    def summed(plan, blocks, valid):
        parts = products(where, plan, blocks)
        parts[1:] = [
            permute(parts[d], lambda at, d=d: dict(x=at["x"] ^ d), valid) for d in (1, 2, 3)
        ]
        return parts

    def settled(parts, valid):
        keep, give = halves(where, parts)
        came = permute(give, lambda at: dict(yl=at["yl"] ^ 1), valid)
        return keep, came

    def home(at):
        z0, y, xh, xl = at["h"] >> 1, at["h"] & 1, at["x"] >> 1, at["x"] & 1
        return dict(h=xh << 1 | y, x=z0 << 1 | xl)

    def flip(at):
        z0, y, xh, xl = at["h"] >> 1, at["h"] & 1, at["x"] >> 1, at["x"] & 1
        return dict(h=z0 << 1 | xl, x=xh << 1 | y)

    moves = lambda at: (at["h"] >> 1) != (at["x"] >> 1)
    own_here, own_there, across = [None] * 3, [None] * SUPERS, [None] * SUPERS

    near = lambda at: True
    blocks = [gradient, y_block, *passing[1:4]]
    first = summed([((0, 1), 0, None, 2), ((0, 1), 3, 2, 4)], blocks, near)
    passing[4], first[1] = lax.optimization_barrier((passing[4], first[1]))
    passing.append(step_on(passing[4], 5))
    keep, came = settled(first, near)
    for k in (0, 1):
        own_here[k] = keep[k] + came[k]
        own_there[k] = permute(own_here[k], home, moves)
        across[k] = permute(
            keep[2 + k] + came[2 + k],
            lambda at, k=k: dict(g=at["g"] - k * way(at), **flip(at)),
            lambda at, k=k: reach(at) >= k and (k > 0 or moves(at) and rank(at) & 1 == 1),
        )

    far = lambda at: reach(at) >= 2
    blocks = [gradient, y_block, end_block, end_y_block, *passing[3:]]
    second = summed([((0, 1), 5, 4, 6), ((2, 3), 5, 4, 6)], blocks, far)
    keep, came = settled(second, far)
    own_here[2] = keep[0] + came[0]
    own_there[2] = permute(own_here[2], home, lambda at: far(at) and moves(at))
    across[2] = permute(
        keep[2] + came[2], lambda at: dict(g=at["g"] - 2 * way(at), **flip(at)), far
    )
    met = lambda at: reach(at) == 2
    own_there[3] = permute(
        keep[1] + came[1], lambda at: dict(g=at["g"] + way(at), **home(at)), met
    )
    across[3] = permute(
        keep[3] + came[3], lambda at: dict(g=at["g"] - 2 * way(at), **flip(at)), met
    )

    mine, given = strips(where, own_here, own_there, across)
    other = permute(given, lambda at: dict(c=at["c"] ^ 1))
    fresh_codes, fresh_scales = refresh(where, mine, other, left_codes[0], left_scales[0])
    return fresh_codes[None], fresh_scales[None]


def solution(mesh):
    return jax.shard_map(
        per_device,
        mesh=mesh,
        in_specs=(P("dp", "tensor"), P("dp", "tensor", None), P("dp", "tensor", None)),
        out_specs=(P("dp", "tensor", None), P("dp", "tensor", None)),
        check_vma=False,
    )
```

```python
import functools

import jax
import jax.numpy as jnp
from jax import lax
from jax.experimental import pallas as pl
from jax.experimental.pallas import tpu as pltpu
from jax.sharding import PartitionSpec as P

GROUP = 128
AXES = ("dp", "tensor")
SUPERS = 4
VMEM = pl.BlockSpec(memory_space=pltpu.VMEM)
SMEM = pl.BlockSpec(memory_space=pltpu.SMEM)


def place(index):
    dp, tensor = divmod(index, 16)
    return dict(
        b=dp >> 4, g=(dp >> 2) & 3, h=dp & 3, x=tensor >> 2, yl=(tensor >> 1) & 1, c=tensor & 1
    )


def index_of(b, g, h, x, yl, c):
    return ((b << 4 | g << 2 | h) << 4) | x << 2 | yl << 1 | c


def permute(array, target, keep=lambda at: True):
    total = lax.axis_size("dp") * lax.axis_size("tensor")
    pairs = []
    for i in range(total):
        at = place(i)
        if keep(at):
            pairs.append((i, index_of(**{**at, **target(at)})))
    return lax.ppermute(array, AXES, pairs)


def reach(at):
    return at["g"] if at["c"] == 0 else SUPERS - 1 - at["g"]


def onward(at):
    return dict(g=at["g"] + (1 if at["c"] == 0 else -1))


def call(kernel, name, outs, flops, *operands):
    in_specs = [SMEM if op.dtype == jnp.int32 else VMEM for op in operands]
    moved = sum(op.size * op.dtype.itemsize for op in (*operands, *outs))
    return pl.pallas_call(
        kernel,
        out_shape=outs,
        in_specs=in_specs,
        out_specs=[VMEM] * len(outs),
        compiler_params=pltpu.CompilerParams(vmem_limit_bytes=40 * 1024 * 1024),
        cost_estimate=pl.CostEstimate(flops=flops, bytes_accessed=moved, transcendentals=0),
        name=name,
    )(*operands)


def floats(*shape):
    return jax.ShapeDtypeStruct(shape, jnp.float32)


def products(rows, cols):
    cols = jnp.concatenate(cols, axis=0)
    return [
        lax.dot_general(
            row, cols, (((1,), (1,)), ((), ())), preferred_element_type=jnp.float32
        )
        for row in rows
    ]


def halves_kernel(far, where, first, second, third, fourth, keep, give):
    half, size = keep.shape[1:]
    upper = where[1] == 1
    total = first[...] + second[...] + third[...] + fourth[...]
    totals = [total[:, k : k + size] for k in range(0, total.shape[1], size)]
    for k, total in enumerate(totals + [totals[k].T for k in far]):
        keep[k] = jnp.where(upper, total[half:], total[:half])
        give[k] = jnp.where(upper, total[:half], total[half:])


def halves(where, far, parts):
    size, width = parts[0].shape
    shape = floats(width // size + len(far), size // 2, size)
    return call(
        functools.partial(halves_kernel, far), "halves", [shape, shape], 0, where, *parts
    )


def strips_kernel(where, *refs):
    own, across, keep, give = refs[:4], (None, *refs[4:7]), refs[7], refs[8]
    half = keep.shape[1]
    second = where[2] == 1
    back = own[3][...] + across[1][...], own[1][...] + across[3][...]
    strips = [
        own[0][...],
        jnp.where(second, back[1], back[0]),
        own[2][...] + across[2][...],
        jnp.where(second, back[0], back[1]),
    ]
    for k, strip in enumerate(strips):
        keep[k] = jnp.where(second, strip[half:], strip[:half])
        give[k] = jnp.where(second, strip[:half], strip[half:])


def strips(where, own, across):
    rows, cols = own[0].shape
    shape = floats(SUPERS, rows // 2, cols)
    return call(strips_kernel, "strips", [shape, shape], 0, where, *own, *across)


def refresh_kernel(where, mine, other, codes, scales, new_codes, new_scales):
    bits = lax.broadcasted_iota(jnp.int32, (GROUP, GROUP), 0) & lax.broadcasted_iota(
        jnp.int32, (GROUP, GROUP), 1
    )
    for shift in (4, 2, 1):
        bits = bits ^ (bits >> shift)
    signs = 1.0 - 2.0 * (bits & 1).astype(jnp.float32)
    unit = 1.0 / (GROUP**0.5)
    per_block = mine.shape[2] // GROUP
    largest = []
    for j in range(SUPERS):
        offset = (j + SUPERS - where[3]) & (SUPERS - 1)
        block = mine[offset] + other[offset]
        for k in range(per_block):
            group = j * per_block + k
            at = slice(group * GROUP, (group + 1) * GROUP)
            turned = jnp.dot(
                block[:, k * GROUP : (k + 1) * GROUP],
                signs,
                precision=lax.Precision.HIGHEST,
                preferred_element_type=jnp.float32,
            )
            old = codes[:, at].astype(jnp.float32) * scales[:, group : group + 1]
            rotated = 0.95 * old + 0.05 * (turned * unit)
            peak = jnp.max(jnp.abs(rotated), axis=1, keepdims=True)
            new_codes[:, at] = (rotated / (peak + 1e-06)).astype(jnp.bfloat16)
            largest.append(peak)
    new_scales[...] = jnp.concatenate(largest, axis=1)


def refresh(where, mine, other, codes, scales):
    return call(
        refresh_kernel,
        "refresh",
        [
            jax.ShapeDtypeStruct(codes.shape, jnp.bfloat16),
            jax.ShapeDtypeStruct(scales.shape, jnp.float32),
        ],
        2 * codes.size * GROUP,
        where,
        mine,
        other,
        codes,
        scales,
    )


def swap_if(flag, first, second):
    return jnp.where(flag, second, first), jnp.where(flag, first, second)


def per_device(gradient, left_codes, left_scales):
    dp, tensor = lax.axis_index("dp"), lax.axis_index("tensor")
    where = jnp.stack(
        [(tensor >> 2) ^ (dp & 3), (tensor >> 1) & 1, tensor & 1, (dp >> 2) & 3]
    ).astype(jnp.int32)

    z_block = permute(gradient, lambda at: dict(h=at["h"] ^ 2))
    y_block = permute(gradient, lambda at: dict(h=at["h"] ^ 1))
    zy_block = permute(z_block, lambda at: dict(h=at["h"] ^ 1))
    turn = (tensor >> 2) ^ (dp & 3)
    low = swap_if(turn & 1 == 1, gradient, y_block)
    high = swap_if(turn & 1 == 1, z_block, zy_block)
    s0, s2 = swap_if(turn >> 1 == 1, low[0], high[0])
    s1, s3 = swap_if(turn >> 1 == 1, low[1], high[1])
    rows = [s0, s1, s2, s3]

    passing = [gradient, permute(gradient, onward, lambda at: reach(at) < 3)]
    passing.append(permute(passing[1], onward, lambda at: 1 <= reach(at) < 3))
    passing.append(
        permute(
            passing[1],
            lambda at: dict(g=at["g"] + (2 if at["c"] == 0 else -2)),
            lambda at: reach(at) == 1,
        )
    )

    own, across = [None] * SUPERS, [None] * SUPERS
    for steps in ((0, 1), (2, 3)):
        parts = products(rows, [passing[step] for step in steps])
        valid = lambda at, steps=steps: reach(at) >= steps[0]
        parts[1:] = [
            permute(parts[d], lambda at, d=d: dict(x=at["x"] ^ d), valid) for d in (1, 2, 3)
        ]
        far = [k for k, step in enumerate(steps) if step]
        keep, give = halves(where, far, parts)
        came = permute(give, lambda at: dict(yl=at["yl"] ^ 1), valid)
        for k, step in enumerate(steps):
            own[step] = keep[k] + came[k]
        for k, place_no in enumerate(far, len(steps)):
            step = steps[place_no]
            across[step] = permute(
                keep[k] + came[k],
                lambda at, step=step: dict(
                    g=at["g"] + (-step if at["c"] == 0 else step), h=at["x"], x=at["h"]
                ),
                lambda at, step=step: reach(at) >= step,
            )

    mine, given = strips(where, own, across[1:])
    other = permute(given, lambda at: dict(c=at["c"] ^ 1))
    fresh_codes, fresh_scales = refresh(where, mine, other, left_codes[0], left_scales[0])
    return fresh_codes[None], fresh_scales[None]


def solution(mesh):
    return jax.shard_map(
        per_device,
        mesh=mesh,
        in_specs=(P("dp", "tensor"), P("dp", "tensor", None), P("dp", "tensor", None)),
        out_specs=(P("dp", "tensor", None), P("dp", "tensor", None)),
        check_vma=False,
    )
```

```python
import functools

import jax
import jax.numpy as jnp
from jax import lax
from jax.experimental import pallas as pl
from jax.experimental.pallas import tpu as pltpu
from jax.sharding import PartitionSpec as P

GROUP = 128
AXES = ("dp", "tensor")
SUPERS = 4
VMEM = pl.BlockSpec(memory_space=pltpu.VMEM)
SMEM = pl.BlockSpec(memory_space=pltpu.SMEM)


def place(index):
    dp, tensor = divmod(index, 16)
    return dict(
        b=dp >> 4, g=(dp >> 2) & 3, h=dp & 3, x=tensor >> 2, yl=(tensor >> 1) & 1, c=tensor & 1
    )


def index_of(b, g, h, x, yl, c):
    return ((b << 4 | g << 2 | h) << 4) | x << 2 | yl << 1 | c


def permute(array, target, keep=lambda at: True):
    total = lax.axis_size("dp") * lax.axis_size("tensor")
    pairs = []
    for i in range(total):
        at = place(i)
        if keep(at):
            pairs.append((i, index_of(**{**at, **target(at)})))
    return lax.ppermute(array, AXES, pairs)


def reach(at):
    return at["g"] if at["c"] == 0 else SUPERS - 1 - at["g"]


def onward(at):
    return dict(g=at["g"] + (1 if at["c"] == 0 else -1))


def call(kernel, name, outs, flops, *operands):
    in_specs = [SMEM if op.dtype == jnp.int32 else VMEM for op in operands]
    moved = sum(op.size * op.dtype.itemsize for op in (*operands, *outs))
    return pl.pallas_call(
        kernel,
        out_shape=outs,
        in_specs=in_specs,
        out_specs=[VMEM] * len(outs),
        compiler_params=pltpu.CompilerParams(vmem_limit_bytes=40 * 1024 * 1024),
        cost_estimate=pl.CostEstimate(flops=flops, bytes_accessed=moved, transcendentals=0),
        name=name,
    )(*operands)


def floats(*shape):
    return jax.ShapeDtypeStruct(shape, jnp.float32)


def products(rows, cols):
    cols = jnp.concatenate(cols, axis=0)
    return [
        lax.dot_general(
            row, cols, (((1,), (1,)), ((), ())), preferred_element_type=jnp.float32
        )
        for row in rows
    ]


def halves_kernel(far, where, first, second, third, fourth, keep, give):
    half, size = keep.shape[1:]
    upper = where[1] == 1
    total = first[...] + second[...] + third[...] + fourth[...]
    totals = [total[:, k : k + size] for k in range(0, total.shape[1], size)]
    for k, total in enumerate(totals + [totals[k].T for k in far]):
        keep[k] = jnp.where(upper, total[half:], total[:half])
        give[k] = jnp.where(upper, total[:half], total[half:])


def halves(where, far, parts):
    size, width = parts[0].shape
    shape = floats(width // size + len(far), size // 2, size)
    return call(
        functools.partial(halves_kernel, far), "halves", [shape, shape], 0, where, *parts
    )


def strips_kernel(where, *refs):
    own, across, keep, give = refs[:4], (None, *refs[4:7]), refs[7], refs[8]
    half = keep.shape[1]
    second = where[2] == 1
    back = own[3][...] + across[1][...], own[1][...] + across[3][...]
    strips = [
        own[0][...],
        jnp.where(second, back[1], back[0]),
        own[2][...] + across[2][...],
        jnp.where(second, back[0], back[1]),
    ]
    for k, strip in enumerate(strips):
        keep[k] = jnp.where(second, strip[half:], strip[:half])
        give[k] = jnp.where(second, strip[:half], strip[half:])


def strips(where, own, across):
    rows, cols = own[0].shape
    shape = floats(SUPERS, rows // 2, cols)
    return call(strips_kernel, "strips", [shape, shape], 0, where, *own, *across)


def refresh_kernel(where, mine, other, codes, scales, new_codes, new_scales):
    bits = lax.broadcasted_iota(jnp.int32, (GROUP, GROUP), 0) & lax.broadcasted_iota(
        jnp.int32, (GROUP, GROUP), 1
    )
    for shift in (4, 2, 1):
        bits = bits ^ (bits >> shift)
    signs = 1.0 - 2.0 * (bits & 1).astype(jnp.float32)
    unit = 1.0 / (GROUP**0.5)
    per_block = mine.shape[2] // GROUP
    largest = []
    for j in range(SUPERS):
        offset = (j + SUPERS - where[3]) & (SUPERS - 1)
        block = mine[offset] + other[offset]
        for k in range(per_block):
            group = j * per_block + k
            at = slice(group * GROUP, (group + 1) * GROUP)
            turned = jnp.dot(
                block[:, k * GROUP : (k + 1) * GROUP],
                signs,
                precision=lax.Precision.HIGHEST,
                preferred_element_type=jnp.float32,
            )
            old = codes[:, at].astype(jnp.float32) * scales[:, group : group + 1]
            rotated = 0.95 * old + 0.05 * (turned * unit)
            peak = jnp.max(jnp.abs(rotated), axis=1, keepdims=True)
            new_codes[:, at] = (rotated / (peak + 1e-06)).astype(jnp.bfloat16)
            largest.append(peak)
    new_scales[...] = jnp.concatenate(largest, axis=1)


def refresh(where, mine, other, codes, scales):
    return call(
        refresh_kernel,
        "refresh",
        [
            jax.ShapeDtypeStruct(codes.shape, jnp.bfloat16),
            jax.ShapeDtypeStruct(scales.shape, jnp.float32),
        ],
        2 * codes.size * GROUP,
        where,
        mine,
        other,
        codes,
        scales,
    )


def swap_if(flag, first, second):
    return jnp.where(flag, second, first), jnp.where(flag, first, second)


def per_device(gradient, left_codes, left_scales):
    dp, tensor = lax.axis_index("dp"), lax.axis_index("tensor")
    where = jnp.stack(
        [(tensor >> 2) ^ (dp & 3), (tensor >> 1) & 1, tensor & 1, (dp >> 2) & 3]
    ).astype(jnp.int32)

    z_block = permute(gradient, lambda at: dict(h=at["h"] ^ 2))
    y_block = permute(gradient, lambda at: dict(h=at["h"] ^ 1))
    zy_block = permute(z_block, lambda at: dict(h=at["h"] ^ 1))
    turn = (tensor >> 2) ^ (dp & 3)
    low = swap_if(turn & 1 == 1, gradient, y_block)
    high = swap_if(turn & 1 == 1, z_block, zy_block)
    s0, s2 = swap_if(turn >> 1 == 1, low[0], high[0])
    s1, s3 = swap_if(turn >> 1 == 1, low[1], high[1])
    rows = [s0, s1, s2, s3]

    passing = [gradient, permute(gradient, onward, lambda at: reach(at) < 3)]
    passing.append(permute(passing[1], onward, lambda at: 1 <= reach(at) < 3))
    passing.append(
        permute(
            passing[1],
            lambda at: dict(g=at["g"] + (2 if at["c"] == 0 else -2)),
            lambda at: reach(at) == 1,
        )
    )

    own, across = [None] * SUPERS, [None] * SUPERS
    for steps in ((0, 1), (2, 3)):
        parts = products(rows, [passing[step] for step in steps])
        valid = lambda at, steps=steps: reach(at) >= steps[0]
        parts[1:] = [
            permute(parts[d], lambda at, d=d: dict(x=at["x"] ^ d), valid) for d in (2, 1, 3)
        ]
        far = [k for k, step in enumerate(steps) if step]
        keep, give = halves(where, far, parts)
        came = permute(give, lambda at: dict(yl=at["yl"] ^ 1), valid)
        for k, step in enumerate(steps):
            own[step] = keep[k] + came[k]
        for k, place_no in enumerate(far, len(steps)):
            step = steps[place_no]
            across[step] = permute(
                keep[k] + came[k],
                lambda at, step=step: dict(
                    g=at["g"] + (-step if at["c"] == 0 else step), h=at["x"], x=at["h"]
                ),
                lambda at, step=step: reach(at) >= step,
            )

    mine, given = strips(where, own, across[1:])
    other = permute(given, lambda at: dict(c=at["c"] ^ 1))
    fresh_codes, fresh_scales = refresh(where, mine, other, left_codes[0], left_scales[0])
    return fresh_codes[None], fresh_scales[None]


def solution(mesh):
    return jax.shard_map(
        per_device,
        mesh=mesh,
        in_specs=(P("dp", "tensor"), P("dp", "tensor", None), P("dp", "tensor", None)),
        out_specs=(P("dp", "tensor", None), P("dp", "tensor", None)),
        check_vma=False,
    )
```

```python
import functools

import jax
import jax.numpy as jnp
from jax import lax
from jax.experimental import pallas as pl
from jax.experimental.pallas import tpu as pltpu
from jax.sharding import PartitionSpec as P

GROUP = 128
AXES = ("dp", "tensor")
SUPERS = 4
VMEM = pl.BlockSpec(memory_space=pltpu.VMEM)
SMEM = pl.BlockSpec(memory_space=pltpu.SMEM)


def place(index):
    dp, tensor = divmod(index, 16)
    return dict(
        b=dp >> 4, g=(dp >> 2) & 3, h=dp & 3, x=tensor >> 2, yl=(tensor >> 1) & 1, c=tensor & 1
    )


def index_of(b, g, h, x, yl, c):
    return ((b << 4 | g << 2 | h) << 4) | x << 2 | yl << 1 | c


def permute(array, target, keep=lambda at: True):
    total = lax.axis_size("dp") * lax.axis_size("tensor")
    pairs = []
    for i in range(total):
        at = place(i)
        if keep(at):
            pairs.append((i, index_of(**{**at, **target(at)})))
    return lax.ppermute(array, AXES, pairs)


def reach(at):
    return at["g"] if at["c"] == 0 else SUPERS - 1 - at["g"]


def way(at):
    return 1 if at["c"] == 0 else -1


def onward(at):
    return dict(g=at["g"] + way(at))


def call(kernel, name, outs, flops, *operands):
    in_specs = [SMEM if op.dtype == jnp.int32 else VMEM for op in operands]
    moved = sum(op.size * op.dtype.itemsize for op in (*operands, *outs))
    return pl.pallas_call(
        kernel,
        out_shape=outs,
        in_specs=in_specs,
        out_specs=[VMEM] * len(outs),
        compiler_params=pltpu.CompilerParams(vmem_limit_bytes=40 * 1024 * 1024),
        cost_estimate=pl.CostEstimate(flops=flops, bytes_accessed=moved, transcendentals=0),
        name=name,
    )(*operands)


def floats(*shape):
    return jax.ShapeDtypeStruct(shape, jnp.float32)


def products(rows, cols):
    cols = jnp.concatenate(cols, axis=0)
    return [
        lax.dot_general(
            row, cols, (((1,), (1,)), ((), ())), preferred_element_type=jnp.float32
        )
        for row in rows
    ]


def halves_kernel(far, where, first, second, third, fourth, keep, give):
    half, size = keep.shape[1:]
    upper = where[0] == 1
    total = first[...] + second[...] + third[...] + fourth[...]
    totals = [total[:, k : k + size] for k in range(0, total.shape[1], size)]
    for k, total in enumerate(totals + [totals[k].T for k in far]):
        keep[k] = jnp.where(upper, total[half:], total[:half])
        give[k] = jnp.where(upper, total[:half], total[half:])


def halves(where, far, parts):
    size, width = parts[0].shape
    shape = floats(width // size + len(far), size // 2, size)
    return call(
        functools.partial(halves_kernel, far), "halves", [shape, shape], 0, where, *parts
    )


def strips_kernel(where, own_0, own_1, across_1, own_late, across_late, keep, give):
    half = keep.shape[1]
    second = where[1] == 1
    reached = jnp.where(second, SUPERS - 1 - where[2], where[2])
    own_two, across_two = reached >= 2, reached <= 1
    none = jnp.zeros_like(own_late)
    mine, others = own_late[...], across_late[...]
    forth = own_1[...] + jnp.where(own_two, none, mine)
    back = across_1[...] + jnp.where(across_two, none, others)
    strips = [
        own_0[...],
        jnp.where(second, forth, back),
        jnp.where(own_two, mine, none) + jnp.where(across_two, others, none),
        jnp.where(second, back, forth),
    ]
    for k, strip in enumerate(strips):
        keep[k] = jnp.where(second, strip[half:], strip[:half])
        give[k] = jnp.where(second, strip[:half], strip[half:])


def strips(where, *parts):
    rows, cols = parts[0].shape
    shape = floats(SUPERS, rows // 2, cols)
    return call(strips_kernel, "strips", [shape, shape], 0, where, *parts)


def refresh_kernel(where, mine, other, codes, scales, new_codes, new_scales):
    bits = lax.broadcasted_iota(jnp.int32, (GROUP, GROUP), 0) & lax.broadcasted_iota(
        jnp.int32, (GROUP, GROUP), 1
    )
    for shift in (4, 2, 1):
        bits = bits ^ (bits >> shift)
    signs = 1.0 - 2.0 * (bits & 1).astype(jnp.float32)
    unit = 1.0 / (GROUP**0.5)
    per_block = mine.shape[2] // GROUP
    largest = []
    for j in range(SUPERS):
        offset = (j + SUPERS - where[2]) & (SUPERS - 1)
        block = mine[offset] + other[offset]
        for k in range(per_block):
            group = j * per_block + k
            at = slice(group * GROUP, (group + 1) * GROUP)
            turned = jnp.dot(
                block[:, k * GROUP : (k + 1) * GROUP],
                signs,
                precision=lax.Precision.HIGHEST,
                preferred_element_type=jnp.float32,
            )
            old = codes[:, at].astype(jnp.float32) * scales[:, group : group + 1]
            rotated = 0.95 * old + 0.05 * (turned * unit)
            peak = jnp.max(jnp.abs(rotated), axis=1, keepdims=True)
            new_codes[:, at] = (rotated / (peak + 1e-06)).astype(jnp.bfloat16)
            largest.append(peak)
    new_scales[...] = jnp.concatenate(largest, axis=1)


def refresh(where, mine, other, codes, scales):
    return call(
        refresh_kernel,
        "refresh",
        [
            jax.ShapeDtypeStruct(codes.shape, jnp.bfloat16),
            jax.ShapeDtypeStruct(scales.shape, jnp.float32),
        ],
        2 * codes.size * GROUP,
        where,
        mine,
        other,
        codes,
        scales,
    )


def swap_if(flag, first, second):
    return jnp.where(flag, second, first), jnp.where(flag, first, second)


def per_device(gradient, left_codes, left_scales):
    dp, tensor = lax.axis_index("dp"), lax.axis_index("tensor")
    core, place_no = tensor & 1, (dp >> 2) & 3
    where = jnp.stack([(tensor >> 1) & 1, core, place_no]).astype(jnp.int32)

    z_block = permute(gradient, lambda at: dict(h=at["h"] ^ 2))
    y_block = permute(gradient, lambda at: dict(h=at["h"] ^ 1))
    zy_block = permute(z_block, lambda at: dict(h=at["h"] ^ 1))
    turn = (tensor >> 2) ^ (dp & 3)
    low = swap_if(turn & 1 == 1, gradient, y_block)
    high = swap_if(turn & 1 == 1, z_block, zy_block)
    s0, s2 = swap_if(turn >> 1 == 1, low[0], high[0])
    s1, s3 = swap_if(turn >> 1 == 1, low[1], high[1])
    rows = [s0, s1, s2, s3]

    passing = permute(gradient, onward, lambda at: reach(at) < 3)
    passing, sent = lax.optimization_barrier((passing, gradient))
    second = permute(passing, onward, lambda at: 1 <= reach(at) < 3)
    opposite = permute(sent, lambda at: dict(g=SUPERS - 1 - at["g"]), lambda at: reach(at) == 3)
    reached = jnp.where(core == 0, place_no, SUPERS - 1 - place_no)
    late = jnp.where(reached >= 2, second, opposite)

    def summed(cols, valid):
        parts = products(rows, cols)
        parts[1:] = [
            permute(parts[d], lambda at, d=d: dict(x=at["x"] ^ d), valid) for d in (2, 1, 3)
        ]
        return parts

    def settle(parts, far, valid):
        keep, give = halves(where, far, parts)
        came = permute(give, lambda at: dict(yl=at["yl"] ^ 1), valid)
        return [keep[k] + came[k] for k in range(keep.shape[0])]

    def back(at):
        g = at["g"]
        return dict(g=SUPERS - 1 - g if reach(at) == 0 else g - 2 * way(at), h=at["x"], x=at["h"])

    early = summed([gradient, passing], lambda at: True)
    late, early[1] = lax.optimization_barrier((late, early[1]))
    valid = lambda at: reach(at) != 1
    last = summed([late], valid)
    last[1], *early = lax.optimization_barrier((last[1], *early))
    own_0, own_1, across_1 = settle(early, (1,), lambda at: True)
    across_1 = permute(
        across_1, lambda at: dict(g=at["g"] - way(at), h=at["x"], x=at["h"]), lambda at: reach(at) > 0
    )
    own_late, across_late = settle(last, (0,), valid)
    across_late = permute(across_late, back, valid)

    mine, given = strips(where, own_0, own_1, across_1, own_late, across_late)
    other = permute(given, lambda at: dict(c=at["c"] ^ 1))
    fresh_codes, fresh_scales = refresh(where, mine, other, left_codes[0], left_scales[0])
    return fresh_codes[None], fresh_scales[None]


def solution(mesh):
    return jax.shard_map(
        per_device,
        mesh=mesh,
        in_specs=(P("dp", "tensor"), P("dp", "tensor", None), P("dp", "tensor", None)),
        out_specs=(P("dp", "tensor", None), P("dp", "tensor", None)),
        check_vma=False,
    )
```

```python
import functools

import jax
import jax.numpy as jnp
from jax import lax
from jax.experimental import pallas as pl
from jax.experimental.pallas import tpu as pltpu
from jax.sharding import PartitionSpec as P

GROUP = 128
AXES = ("dp", "tensor")
SUPERS = 4
VMEM = pl.BlockSpec(memory_space=pltpu.VMEM)
SMEM = pl.BlockSpec(memory_space=pltpu.SMEM)


def place(index):
    dp, tensor = divmod(index, 16)
    return dict(
        b=dp >> 4, g=(dp >> 2) & 3, h=dp & 3, x=tensor >> 2, yl=(tensor >> 1) & 1, c=tensor & 1
    )


def index_of(b, g, h, x, yl, c):
    return ((b << 4 | g << 2 | h) << 4) | x << 2 | yl << 1 | c


def permute(array, target, keep=lambda at: True):
    total = lax.axis_size("dp") * lax.axis_size("tensor")
    pairs = []
    for i in range(total):
        at = place(i)
        if keep(at):
            pairs.append((i, index_of(**{**at, **target(at)})))
    return lax.ppermute(array, AXES, pairs)


def reach(at):
    return at["g"] if at["c"] == 0 else SUPERS - 1 - at["g"]


def onward(at):
    return dict(g=at["g"] + (1 if at["c"] == 0 else -1))


def call(kernel, name, outs, flops, *operands):
    in_specs = [SMEM if op.dtype == jnp.int32 else VMEM for op in operands]
    moved = sum(op.size * op.dtype.itemsize for op in (*operands, *outs))
    return pl.pallas_call(
        kernel,
        out_shape=outs,
        in_specs=in_specs,
        out_specs=[VMEM] * len(outs),
        compiler_params=pltpu.CompilerParams(vmem_limit_bytes=40 * 1024 * 1024),
        cost_estimate=pl.CostEstimate(flops=flops, bytes_accessed=moved, transcendentals=0),
        name=name,
    )(*operands)


def floats(*shape):
    return jax.ShapeDtypeStruct(shape, jnp.float32)


def products(rows, cols):
    cols = jnp.concatenate(cols, axis=0)
    return [
        lax.dot_general(
            row, cols, (((1,), (1,)), ((), ())), preferred_element_type=jnp.float32
        )
        for row in rows
    ]


def halves_kernel(far, where, first, second, third, fourth, keep, give):
    half, size = keep.shape[1:]
    upper = where[1] == 1
    total = first[...] + second[...] + third[...] + fourth[...]
    totals = [total[:, k : k + size] for k in range(0, total.shape[1], size)]
    for k, total in enumerate(totals + [totals[k].T for k in far]):
        keep[k] = jnp.where(upper, total[half:], total[:half])
        give[k] = jnp.where(upper, total[:half], total[half:])


def halves(where, far, parts):
    size, width = parts[0].shape
    shape = floats(width // size + len(far), size // 2, size)
    return call(
        functools.partial(halves_kernel, far), "halves", [shape, shape], 0, where, *parts
    )


def strips_kernel(where, *refs):
    own, across, keep, give = refs[:4], (None, *refs[4:7]), refs[7], refs[8]
    half = keep.shape[1]
    second = where[2] == 1
    back = own[3][...] + across[1][...], own[1][...] + across[3][...]
    strips = [
        own[0][...],
        jnp.where(second, back[1], back[0]),
        own[2][...] + across[2][...],
        jnp.where(second, back[0], back[1]),
    ]
    for k, strip in enumerate(strips):
        keep[k] = jnp.where(second, strip[half:], strip[:half])
        give[k] = jnp.where(second, strip[:half], strip[half:])


def strips(where, own, across):
    rows, cols = own[0].shape
    shape = floats(SUPERS, rows // 2, cols)
    return call(strips_kernel, "strips", [shape, shape], 0, where, *own, *across)


def refresh_kernel(where, mine, other, codes, scales, new_codes, new_scales):
    bits = lax.broadcasted_iota(jnp.int32, (GROUP, GROUP), 0) & lax.broadcasted_iota(
        jnp.int32, (GROUP, GROUP), 1
    )
    for shift in (4, 2, 1):
        bits = bits ^ (bits >> shift)
    signs = 1.0 - 2.0 * (bits & 1).astype(jnp.float32)
    unit = 1.0 / (GROUP**0.5)
    per_block = mine.shape[2] // GROUP
    largest = []
    for j in range(SUPERS):
        offset = (j + SUPERS - where[3]) & (SUPERS - 1)
        block = mine[offset] + other[offset]
        for k in range(per_block):
            group = j * per_block + k
            at = slice(group * GROUP, (group + 1) * GROUP)
            turned = jnp.dot(
                block[:, k * GROUP : (k + 1) * GROUP],
                signs,
                precision=lax.Precision.HIGHEST,
                preferred_element_type=jnp.float32,
            )
            old = codes[:, at].astype(jnp.float32) * scales[:, group : group + 1]
            rotated = 0.95 * old + 0.05 * (turned * unit)
            peak = jnp.max(jnp.abs(rotated), axis=1, keepdims=True)
            new_codes[:, at] = (rotated / (peak + 1e-06)).astype(jnp.bfloat16)
            largest.append(peak)
    new_scales[...] = jnp.concatenate(largest, axis=1)


def refresh(where, mine, other, codes, scales):
    return call(
        refresh_kernel,
        "refresh",
        [
            jax.ShapeDtypeStruct(codes.shape, jnp.bfloat16),
            jax.ShapeDtypeStruct(scales.shape, jnp.float32),
        ],
        2 * codes.size * GROUP,
        where,
        mine,
        other,
        codes,
        scales,
    )


def swap_if(flag, first, second):
    return jnp.where(flag, second, first), jnp.where(flag, first, second)


def per_device(gradient, left_codes, left_scales):
    dp, tensor = lax.axis_index("dp"), lax.axis_index("tensor")
    where = jnp.stack(
        [(tensor >> 2) ^ (dp & 3), (tensor >> 1) & 1, tensor & 1, (dp >> 2) & 3]
    ).astype(jnp.int32)

    z_block = permute(gradient, lambda at: dict(h=at["h"] ^ 2))
    y_block = permute(gradient, lambda at: dict(h=at["h"] ^ 1))
    zy_block = permute(z_block, lambda at: dict(h=at["h"] ^ 1))
    turn = (tensor >> 2) ^ (dp & 3)
    low = swap_if(turn & 1 == 1, gradient, y_block)
    high = swap_if(turn & 1 == 1, z_block, zy_block)
    s0, s2 = swap_if(turn >> 1 == 1, low[0], high[0])
    s1, s3 = swap_if(turn >> 1 == 1, low[1], high[1])
    s1, s3 = swap_if(tensor & 1 == 1, s1, s3)
    rows = [s0, s1, s2, s3]

    passing = [gradient, permute(gradient, onward, lambda at: reach(at) < 3)]
    passing.append(permute(passing[1], onward, lambda at: 1 <= reach(at) < 3))
    passing.append(
        permute(
            passing[1],
            lambda at: dict(g=at["g"] + (2 if at["c"] == 0 else -2)),
            lambda at: reach(at) == 1,
        )
    )

    own, across = [None] * SUPERS, [None] * SUPERS
    for steps in ((0, 1), (2, 3)):
        parts = products(rows, [passing[step] for step in steps])
        valid = lambda at, steps=steps: reach(at) >= steps[0]
        parts[1:] = [
            permute(parts[d], lambda at, d=d: dict(x=at["x"] ^ (d if at["c"] == 0 else -d & 3)), valid) for d in (2, 1, 3)
        ]
        far = [k for k, step in enumerate(steps) if step]
        keep, give = halves(where, far, parts)
        came = permute(give, lambda at: dict(yl=at["yl"] ^ 1), valid)
        for k, step in enumerate(steps):
            own[step] = keep[k] + came[k]
        for k, place_no in enumerate(far, len(steps)):
            step = steps[place_no]
            across[step] = permute(
                keep[k] + came[k],
                lambda at, step=step: dict(
                    g=at["g"] + (-step if at["c"] == 0 else step), h=at["x"], x=at["h"]
                ),
                lambda at, step=step: reach(at) >= step,
            )

    mine, given = strips(where, own, across[1:])
    other = permute(given, lambda at: dict(c=at["c"] ^ 1))
    fresh_codes, fresh_scales = refresh(where, mine, other, left_codes[0], left_scales[0])
    return fresh_codes[None], fresh_scales[None]


def solution(mesh):
    return jax.shard_map(
        per_device,
        mesh=mesh,
        in_specs=(P("dp", "tensor"), P("dp", "tensor", None), P("dp", "tensor", None)),
        out_specs=(P("dp", "tensor", None), P("dp", "tensor", None)),
        check_vma=False,
    )
```
